32 devices in a mesh: seed: 4 (over z), tok: 8 (over y, x, core).
Axes of the slice: x: 2, y: 2, z: 4, core: 2. Of those that a mesh axis runs over, the one named last changes fastest.
Arguments:
- atom_single: bfloat16 [8192, 128], P(('seed', 'tok')), parts along dimension 0, may hold values from -6 to 6
- atom_bias: bfloat16 [2048, 512], P('tok'), may hold values from -400 to 400
- atom_token: int32 [2048], P('tok'), may hold values from 0 to 255, as said below
- atom_counts: int32 [256], P('tok'), may hold values from 1 to 15, as said below
- pair_rep: bfloat16 [256, 256, 128], P('tok'), may hold values from -400 to 400
- atom_qkv_w: bfloat16 [128, 384], replicated, may hold values from -0.5 to 0.5
- atom_out_w: bfloat16 [128, 128], replicated, may hold values from -0.5 to 0.5
- agg_w: bfloat16 [128, 768], replicated, may hold values from -0.5 to 0.5
- tok_qkv_w: bfloat16 [2, 768, 2304], replicated, may hold values from -0.21875 to 0.21875
- tok_out_w: bfloat16 [2, 768, 768], replicated, may hold values from -0.4375 to 0.4375
- pair_w: bfloat16 [128, 32], replicated, may hold values from -0.5 to 0.5
- bcast_w: bfloat16 [768, 128], replicated, may hold values from -0.21875 to 0.21875
Outputs:
- atom_out: bfloat16 [8192, 128], P(('seed', 'tok')), parts along dimension 0
- token_out: bfloat16 [1024, 768], P(('seed', 'tok')), parts along dimension 0
The draws below stay inside these ranges and needn't reach their ends.
There are 4 independent parts, one for each index of `seed`. The reference program is written for one: setup_inputs(seed, part) draws one part's arguments, and reference() takes and returns one part's arrays. A program takes and returns all parts, laid end to end along the dimension named above; an argument that names none is the same for every part. Nothing has to cross between parts.
Inputs may be any that keep to these rules, and one draw needn't show every extreme that they name: `atom_counts`: counts sum to 2048; the counts of the tokens of one index of tok sum to 256; the largest count is 15 and the smallest 1 in every draw. `atom_token`: token t holds exactly atom_counts[t] atoms, and the atoms of one token are consecutive. Along the atoms the tokens come in increasing order, except that at each boundary between neighbouring indices of tok the first token of the upper index comes just before the last token of the lower index; so every atom belongs to a token of its own index of tok or of a neighbouring one.
All inputs are finite; a program needn't handle non-finite values.
Results may differ from the reference program's by a relative error of at most 0.017.
Values may be sent and summed in bfloat16 or wider, within the bound.
A program may use at most 128 MiB of HBM per device.

```python
import jax
import jax.numpy as jnp
from jax import lax

C = 768
H = 16
CZ = 128
CA = 128
AH = 4
QW = 32
KW = 128
ATOMS_PER_TOKEN = 8
NB = 2
TOK_DEV = 32
TOKENS = 256
ATOMS = 2048
HALO = 48
N_TOK = 8


def atom_layout(key):
    jitter = jax.random.randint(key, (TOKENS // 2,), -3, 4)
    jitter = jitter.at[0].set(ATOMS_PER_TOKEN - 1)
    counts = jnp.stack([ATOMS_PER_TOKEN + jitter, ATOMS_PER_TOKEN - jitter], axis=1).reshape(TOKENS).astype(jnp.int32)
    lower = jnp.arange(N_TOK - 1, dtype=jnp.int32) * TOK_DEV + TOK_DEV - 1
    upper = lower + 1
    order = jnp.arange(TOKENS, dtype=jnp.int32)
    order = order.at[lower].set(upper).at[upper].set(lower)
    ends = jnp.cumsum(counts[order]).astype(jnp.int32)
    place = jnp.searchsorted(ends, jnp.arange(ATOMS, dtype=jnp.int32), side='right')
    owner = order[place]
    return (counts, owner.astype(jnp.int32))


def draw_atom_counts(key, part):
    counts, owner = atom_layout(key)
    return counts


def draw_atom_token(key, part):
    counts, owner = atom_layout(key)
    return owner


def draw_atom_bias(key, part):
    key = jax.random.fold_in(key, 11)
    key_base = jax.random.fold_in(key, 0)
    base = jnp.clip(jax.random.normal(key_base, (ATOMS, AH * KW), jnp.float32), -6.0, 6.0)
    return base.astype(jnp.bfloat16)


def draw_pair_rep(key, part):
    key = jax.random.fold_in(key, 23)
    key_base = jax.random.fold_in(key, 0)
    base = jnp.clip(jax.random.normal(key_base, (TOKENS, TOKENS, CZ), jnp.float32), -6.0, 6.0)
    return base.astype(jnp.bfloat16)


def levels(key, extent, cuts, least, largest):
    def one(dim, blocks):
        steps = jax.random.uniform(jax.random.fold_in(jax.random.fold_in(key, 6), dim), (blocks,), jnp.float32, least / len(cuts), largest / len(cuts))
        return jnp.repeat(jnp.exp(steps), extent[dim] // blocks).reshape((-1,) + (1,) * (len(extent) - dim - 1))

    level = one(*cuts[0])
    for cut in cuts[1:]:
        level = level * one(*cut)
    return level


def gaussian(stream_key, extent, spread, limit, pieces=(), held_as=jnp.bfloat16):
    entries = spread * jax.random.normal(stream_key, extent, jnp.float32)
    if pieces:
        entries = entries * levels(stream_key, extent, pieces, -0.22, 0.18)
    return jnp.clip(entries, -limit, limit).astype(held_as)


def setup_inputs(seed: int = 0, part: int = 0) -> dict:
    splits = jax.random.split(jax.random.key(seed), 13)
    part_keys = jax.random.split(jax.random.fold_in(splits[12], part), 13)
    return {
        "atom_single": gaussian(part_keys[0], (ATOMS, CA), 1.0, 6.0, ((0, 8),)),
        "atom_bias": draw_atom_bias(jax.random.fold_in(splits[12], 71), part),
        "atom_token": draw_atom_token(jax.random.fold_in(splits[12], 71), part),
        "atom_counts": draw_atom_counts(jax.random.fold_in(splits[12], 71), part),
        "pair_rep": draw_pair_rep(jax.random.fold_in(splits[12], 71), part),
        "atom_qkv_w": gaussian(splits[5], (CA, 3 * CA), CA ** -0.5, 0.5),
        "atom_out_w": gaussian(splits[6], (CA, CA), CA ** -0.5, 0.5),
        "agg_w": gaussian(splits[7], (CA, C), CA ** -0.5, 0.5),
        "tok_qkv_w": gaussian(splits[8], (NB, C, 3 * C), C ** -0.5, 0.21875),
        "tok_out_w": gaussian(splits[9], (NB, C, C), (C // 4) ** -0.5, 0.4375),
        "pair_w": gaussian(splits[10], (CZ, NB * H), CZ ** -0.5, 0.5),
        "bcast_w": gaussian(splits[11], (C, CA), C ** -0.5, 0.21875),
    }


def layer_norm(values):
    average = lax.optimization_barrier(jnp.mean(values, axis=-1, keepdims=True))
    centred = values - average
    variance = lax.optimization_barrier(jnp.mean(centred * centred, axis=-1, keepdims=True))
    return centred * lax.rsqrt(variance + 1e-05)

def window_attend(queries, keyvals, atom_bias, first_atom, atom_total):
    windows = keyvals.shape[0]
    head_width = CA // AH
    query_heads = queries.reshape(windows, QW, AH, head_width).astype(jnp.float32)
    key_heads = keyvals[:, :, :CA].reshape(windows, KW, AH, head_width).astype(jnp.float32)
    value_heads = keyvals[:, :, CA:].reshape(windows, KW, AH, head_width).astype(jnp.float32)
    scores = jnp.einsum('wqhd,wkhd->whqk', query_heads, key_heads) * head_width ** (-0.5)
    scores = scores + atom_bias.reshape(windows, QW, AH, KW).transpose(0, 2, 1, 3).astype(jnp.float32)
    position = first_atom + QW * jnp.arange(windows, dtype=jnp.int32)[:, None] - HALO + jnp.arange(KW, dtype=jnp.int32)[None, :]
    inside = (position >= 0) & (position < atom_total)
    scores = jnp.where(inside[:, None, None, :], scores, -1000000000.0)
    maximum = lax.optimization_barrier(jnp.max(scores, axis=-1, keepdims=True))
    powers = jnp.exp(scores - maximum)
    denominator = lax.optimization_barrier(jnp.sum(powers, axis=-1))
    weights = lax.optimization_barrier(powers.astype(jnp.bfloat16)).astype(jnp.float32)
    mixed_heads = jnp.einsum('whqk,wkhd->wqhd', weights, value_heads) / denominator.transpose(0, 2, 1)[..., None]
    return mixed_heads.reshape(windows * QW, CA).astype(jnp.bfloat16)

def reference(atom_single, atom_bias, atom_token, atom_counts, pair_rep, atom_qkv_w, atom_out_w, agg_w, tok_qkv_w, tok_out_w, pair_w, bcast_w):
    hidden_in = atom_single.astype(jnp.float32)
    normed = layer_norm(hidden_in).astype(jnp.bfloat16)
    projected = jnp.dot(normed, atom_qkv_w, preferred_element_type=jnp.float32).astype(jnp.bfloat16)
    queries = projected[:, :CA]
    padded = jnp.pad(projected[:, CA:], ((HALO, HALO), (0, 0)))
    windows = ATOMS // QW
    gather_index = QW * jnp.arange(windows, dtype=jnp.int32)[:, None] + jnp.arange(KW, dtype=jnp.int32)[None, :]
    keyvals = padded[gather_index]
    attended = window_attend(queries, keyvals, atom_bias, 0, ATOMS)
    atom_hidden = (hidden_in + jnp.dot(attended, atom_out_w, preferred_element_type=jnp.float32)).astype(jnp.bfloat16)
    lifted = jax.nn.relu(jnp.dot(atom_hidden, agg_w, preferred_element_type=jnp.float32))
    token_sums = jax.ops.segment_sum(lifted, atom_token, num_segments=TOKENS)
    stream = token_sums / atom_counts.astype(jnp.float32)[:, None]

    def project_rows(row_block):
        return jnp.einsum('ijc,ch->hij', row_block.astype(jnp.float32), pair_w.astype(jnp.float32)).astype(jnp.bfloat16)
    pair_bias = lax.map(project_rows, pair_rep.reshape(N_TOK, TOK_DEV, TOKENS, CZ))
    pair_bias = pair_bias.transpose(1, 0, 2, 3).reshape(NB * H, TOKENS, TOKENS)
    head_size = C // H

    def one_head(operands):
        query_rows, key_rows, value_rows, bias_rows = operands
        scores = jnp.dot(query_rows, key_rows.T, preferred_element_type=jnp.float32) * head_size ** (-0.5)
        scores = scores + bias_rows.astype(jnp.float32)
        maximum = lax.optimization_barrier(jnp.max(scores, axis=-1, keepdims=True))
        powers = jnp.exp(scores - maximum)
        denominator = lax.optimization_barrier(jnp.sum(powers, axis=-1))
        weights = powers.astype(jnp.bfloat16)
        return jnp.dot(weights, value_rows, preferred_element_type=jnp.float32) / denominator[:, None]
    for layer_index in range(NB):
        normed = layer_norm(stream).astype(jnp.bfloat16)
        projected = jnp.dot(normed, tok_qkv_w[layer_index], preferred_element_type=jnp.float32).astype(jnp.bfloat16)
        query_heads = projected[:, :C].reshape(TOKENS, H, head_size).transpose(1, 0, 2)
        key_heads = projected[:, C:2 * C].reshape(TOKENS, H, head_size).transpose(1, 0, 2)
        value_heads = projected[:, 2 * C:].reshape(TOKENS, H, head_size).transpose(1, 0, 2)
        bias_layer = pair_bias[layer_index * H:(layer_index + 1) * H]
        mixed_heads = lax.map(one_head, (query_heads, key_heads, value_heads, bias_layer))
        mixed_heads = mixed_heads.transpose(1, 0, 2).reshape(TOKENS, C).astype(jnp.bfloat16)
        stream = stream + jnp.dot(mixed_heads, tok_out_w[layer_index], preferred_element_type=jnp.float32)
    token_out = stream.astype(jnp.bfloat16)
    token_carry = jnp.dot(token_out, bcast_w, preferred_element_type=jnp.float32).astype(jnp.bfloat16)
    picked = jnp.take(token_carry, atom_token, axis=0)
    atom_out = (atom_hidden.astype(jnp.float32) + picked.astype(jnp.float32)).astype(jnp.bfloat16)
    return (atom_out, token_out)
```

```python
import functools

import jax
import jax.numpy as jnp
from jax import lax
from jax.experimental import pallas as pl
from jax.experimental.pallas import tpu as pltpu
from jax.sharding import PartitionSpec as P

H = 16
AH = 4
QW = 32
KW = 128
HALO = 48
SIDE = QW + HALO
EXTRA = 16
F32 = jnp.float32
BF16 = jnp.bfloat16


def layer_norm(values):
    average = jnp.mean(values, axis=-1, keepdims=True)
    centred = values - average
    variance = jnp.mean(centred * centred, axis=-1, keepdims=True)
    return centred * lax.rsqrt(variance + 1e-05)


def dot(a, b):
    return jnp.dot(a, b, preferred_element_type=F32)


def dot_nt(a, b):
    return lax.dot_general(a, b, (((1,), (1,)), ((), ())), preferred_element_type=F32)


def dot_tn(a, b):
    return lax.dot_general(a, b, (((0,), (0,)), ((), ())), preferred_element_type=F32)


def wanted_tokens(tokens, count):
    first = lax.axis_index("tok") * tokens
    row = lax.broadcasted_iota(jnp.int32, (count, 1), 0)
    sides = jnp.where(row == tokens, first - 1, jnp.where(row == tokens + 1, first + tokens, -9))
    return jnp.where(row < tokens, first + row, sides)


def kernel(
    n,
    single_hbm,
    bias_hbm,
    token_hbm,
    pair_hbm,
    qkv_hbm,
    aout_hbm,
    agg_hbm,
    tqkv_hbm,
    tout_hbm,
    pairw_hbm,
    hidden_out,
    final_out,
    xs,
    bs,
    tok_mid,
    tok_low,
    tok_high,
    pair,
    qkv_w,
    aout_w,
    agg_w,
    tqkv_w,
    tout_w,
    pair_w,
    proj,
    mixed,
    gathered,
    pbias,
    local_sem,
    halo_send,
    halo_recv,
    gather_send,
    gather_recv,
):
    atoms, ca = single_hbm.shape
    tokens = pair_hbm.shape[0]
    blocks, c, _ = tout_hbm.shape
    all_tokens = n * tokens
    ext_atoms = atoms + 2 * QW
    ext_tokens = tokens + EXTRA
    used = tokens + 2
    me = lax.axis_index("tok")
    right = lax.rem(me + 1, n)
    left = lax.rem(me + n - 1, n)

    barrier = pltpu.get_barrier_semaphore()
    for k in range(1, n):
        pl.semaphore_signal(
            barrier,
            inc=1,
            device_id={"tok": lax.rem(me + k, n)},
            device_id_type=pl.DeviceIdType.MESH,
        )

    moves = [
        (single_hbm, xs.at[SIDE : SIDE + atoms]),
        (bias_hbm, bs.at[QW : QW + atoms]),
        (token_hbm, tok_mid),
        (qkv_hbm, qkv_w),
        (aout_hbm, aout_w),
        (agg_hbm, agg_w),
        (pairw_hbm, pair_w),
        (pair_hbm, pair.at[0:tokens]),
        (tqkv_hbm.at[0], tqkv_w.at[0]),
        (tout_hbm.at[0], tout_w.at[0]),
        (tqkv_hbm.at[1], tqkv_w.at[1]),
        (tout_hbm.at[1], tout_w.at[1]),
    ]
    copies = [
        pltpu.make_async_copy(src, dst, local_sem.at[i]) for i, (src, dst) in enumerate(moves)
    ]
    for copy in copies[:8]:
        copy.start()
    (c_single, c_bias, c_token, c_qkv, c_aout, c_agg, c_pairw, c_pair) = copies[:8]
    c_tqkv = [copies[8], copies[10]]
    c_tout = [copies[9], copies[11]]

    pl.semaphore_wait(barrier, n - 1)
    halo_moves = [
        (single_hbm.at[atoms - SIDE : atoms], xs.at[0:SIDE], right),
        (single_hbm.at[0:SIDE], xs.at[SIDE + atoms : 2 * SIDE + atoms], left),
        (bias_hbm.at[atoms - QW : atoms], bs.at[0:QW], right),
        (bias_hbm.at[0:QW], bs.at[QW + atoms : 2 * QW + atoms], left),
        (token_hbm, tok_low, right),
        (token_hbm, tok_high, left),
        (pair_hbm.at[tokens - 1], pair.at[tokens], right),
        (pair_hbm.at[0], pair.at[tokens + 1], left),
    ]
    halos = [
        pltpu.make_async_remote_copy(
            src_ref=src,
            dst_ref=dst,
            send_sem=halo_send.at[i],
            recv_sem=halo_recv.at[i],
            device_id={"tok": to},
            device_id_type=pl.DeviceIdType.MESH,
        )
        for i, (src, dst, to) in enumerate(halo_moves)
    ]
    for copy in halos:
        copy.start()
    for copy in copies[8:]:
        copy.start()

    def pair_rows(t):
        rows = dot_nt(pair_w[...], pair[t]).astype(BF16)
        for b in range(blocks):
            pbias[b, t * H : (t + 1) * H, :] = rows[b * H : (b + 1) * H]

    c_single.wait()
    c_bias.wait()
    c_token.wait()
    c_qkv.wait()
    width = ca // AH
    lane = lax.broadcasted_iota(jnp.int32, (QW, ca), 1)
    head_masks = [(lane // width == h).astype(F32) for h in range(AH)]
    head_picks = [m.astype(BF16) for m in head_masks]
    key_lane = lax.broadcasted_iota(jnp.int32, (1, KW), 1)

    def project(rows):
        return dot(layer_norm(rows.astype(F32)).astype(BF16), qkv_w[...]).astype(BF16)

    def window(w):
        q = proj[HALO + QW * w : HALO + QW * (w + 1), :ca]
        keys = proj[QW * w : QW * w + KW, ca : 2 * ca]
        values = proj[QW * w : QW * w + KW, 2 * ca :]
        spread = jnp.concatenate([q * pick for pick in head_picks], axis=0)
        bias = jnp.concatenate(
            [bs[QW * w : QW * (w + 1), h * KW : (h + 1) * KW] for h in range(AH)], axis=0
        )
        scores = dot_nt(spread, keys) * width ** (-0.5) + bias.astype(F32)
        position = me * atoms - SIDE + QW * w + key_lane
        inside = (position >= 0) & (position < n * atoms)
        scores = jnp.where(inside, scores, -1000000000.0)
        powers = jnp.exp(scores - jnp.max(scores, axis=-1, keepdims=True))
        total = jnp.sum(powers, axis=-1, keepdims=True)
        heads = dot(powers.astype(BF16), values) / total
        out = heads[:QW] * head_masks[0]
        for h in range(1, AH):
            out = out + heads[h * QW : (h + 1) * QW] * head_masks[h]
        mixed[QW * w : QW * (w + 1), :] = out.astype(BF16)

    windows = range(ext_atoms // QW)
    inner = [w for w in windows if QW * w >= SIDE and QW * w + KW <= SIDE + atoms]
    proj[SIDE : SIDE + atoms, :] = project(xs[SIDE : SIDE + atoms])
    for w in inner:
        window(w)
    for copy in halos[:6]:
        copy.wait()
    edges = project(jnp.concatenate([xs[:SIDE], xs[SIDE + atoms :]], axis=0))
    proj[:SIDE, :] = edges[:SIDE]
    proj[SIDE + atoms :, :] = edges[SIDE:]
    for w in windows:
        if w not in inner:
            window(w)
    c_aout.wait()
    c_agg.wait()
    own_rows = xs[HALO : HALO + ext_atoms].astype(F32)
    hidden = (own_rows + dot(mixed[...], aout_w[...])).astype(BF16)
    hidden_out[...] = hidden[QW : QW + atoms]
    lifted = jnp.maximum(dot(hidden, agg_w[...]), 0.0)

    wanted = wanted_tokens(tokens, ext_tokens)
    near = jnp.concatenate(
        [tok_low[:, atoms - QW :], tok_mid[...], tok_high[:, :QW]], axis=1
    )
    member = (near == wanted).astype(F32)
    count = jnp.maximum(jnp.sum(member, axis=-1, keepdims=True), 1.0)
    picker = member.astype(BF16)
    upper = lifted.astype(BF16)
    lower = (lifted - upper.astype(F32)).astype(BF16)
    stream = (dot(picker, upper) + dot(picker, lower)) / count

    rows = used * H
    head_size = c // H
    row_token = lax.broadcasted_iota(jnp.int32, (rows, ext_tokens), 0) // H
    spreader = (row_token == lax.broadcasted_iota(jnp.int32, (rows, ext_tokens), 1)).astype(
        F32
    ).astype(BF16)
    col_token = lax.broadcasted_iota(jnp.int32, (ext_tokens, rows), 1) // H
    collector = (col_token == lax.broadcasted_iota(jnp.int32, (ext_tokens, rows), 0)).astype(
        F32
    ).astype(BF16)
    head_row = lax.broadcasted_iota(jnp.int32, (H, c), 0)
    head_lane = lax.broadcasted_iota(jnp.int32, (H, c), 1) // head_size
    tok_mask = (head_row == head_lane).astype(F32).astype(BF16)
    tok_mask = jnp.concatenate([tok_mask] * used, axis=0)
    own = pl.ds(pl.multiple_of(me * tokens, tokens), tokens)
    for b in range(blocks):
        normed = layer_norm(stream).astype(BF16)
        gathered[b, own, :] = normed[:tokens]
        sends = [
            pltpu.make_async_remote_copy(
                src_ref=gathered.at[b, own],
                dst_ref=gathered.at[b, own],
                send_sem=gather_send.at[b, k - 1],
                recv_sem=gather_recv.at[b, k - 1],
                device_id={"tok": lax.rem(me + k, n)},
                device_id_type=pl.DeviceIdType.MESH,
            )
            for k in range(1, n)
        ]
        for copy in sends:
            copy.start()
        if b == 0:
            c_pairw.wait()
            c_pair.wait()
            for copy in halos[6:]:
                copy.wait()
            for t in range(used):
                pair_rows(t)
        c_tqkv[b].wait()
        q = dot(normed, tqkv_w[b, :, :c]).astype(BF16)
        spread = dot(spreader, q).astype(BF16) * tok_mask
        c_tout[b].wait()
        for copy in sends:
            copy.wait()
        everyone = gathered[b]
        keys = dot(everyone, tqkv_w[b, :, c : 2 * c]).astype(BF16)
        scores = dot_nt(spread, keys) * head_size ** (-0.5) + pbias[b].astype(F32)
        powers = jnp.exp(scores - jnp.max(scores, axis=-1, keepdims=True))
        total = jnp.sum(powers, axis=-1, keepdims=True)
        values = dot(everyone, tqkv_w[b, :, 2 * c :]).astype(BF16)
        heads = (dot(powers.astype(BF16), values) / total).astype(BF16) * tok_mask
        mixed = dot(collector, heads).astype(BF16)
        stream = stream + dot(mixed, tout_w[b])

    final_out[...] = stream.astype(BF16)


def hand_over(final, hidden, token, bcast, atom_out, token_out):
    tokens = token_out.shape[0]
    token_out[...] = final[:tokens, :]
    carry = dot(final[...], bcast[...]).astype(BF16)
    mine = (token[...] == wanted_tokens(tokens, final.shape[0])).astype(F32).astype(BF16)
    atom_out[...] = (hidden[...].astype(F32) + dot_tn(mine, carry)).astype(BF16)


def local(
    atom_single,
    atom_bias,
    atom_token,
    atom_counts,
    pair_rep,
    atom_qkv_w,
    atom_out_w,
    agg_w,
    tok_qkv_w,
    tok_out_w,
    pair_w,
    bcast_w,
):
    n = lax.axis_size("tok")
    atoms, ca = atom_single.shape
    tokens, all_tokens, cz = pair_rep.shape
    blocks, c, _ = tok_out_w.shape
    operands = (
        atom_single,
        atom_bias,
        atom_token.reshape(1, atoms),
        pair_rep,
        atom_qkv_w,
        atom_out_w,
        agg_w,
        tok_qkv_w,
        tok_out_w,
        pair_w.T,
    )
    dma = pltpu.SemaphoreType.DMA
    hidden, final = pl.pallas_call(
        functools.partial(kernel, n),
        out_shape=(
            pltpu.VMEM((atoms, ca), BF16),
            pltpu.VMEM((tokens + EXTRA, c), BF16),
        ),
        in_specs=[pl.BlockSpec(memory_space=pltpu.HBM)] * len(operands),
        out_specs=(pl.BlockSpec(memory_space=pltpu.VMEM),) * 2,
        scratch_shapes=[
            pltpu.VMEM((atoms + 2 * SIDE, ca), BF16),
            pltpu.VMEM((atoms + 2 * QW, AH * KW), BF16),
            pltpu.VMEM((1, atoms), jnp.int32),
            pltpu.VMEM((1, atoms), jnp.int32),
            pltpu.VMEM((1, atoms), jnp.int32),
            pltpu.VMEM((tokens + 2, all_tokens, cz), BF16),
            pltpu.VMEM(atom_qkv_w.shape, BF16),
            pltpu.VMEM(atom_out_w.shape, BF16),
            pltpu.VMEM(agg_w.shape, BF16),
            pltpu.VMEM(tok_qkv_w.shape, BF16),
            pltpu.VMEM(tok_out_w.shape, BF16),
            pltpu.VMEM(pair_w.shape[::-1], BF16),
            pltpu.VMEM((atoms + 2 * SIDE, 3 * ca), BF16),
            pltpu.VMEM((atoms + 2 * QW, ca), BF16),
            pltpu.VMEM((blocks, all_tokens, c), BF16),
            pltpu.VMEM((blocks, (tokens + 2) * H, all_tokens), BF16),
            dma((12,)),
            dma((8,)),
            dma((8,)),
            dma((blocks, n - 1)),
            dma((blocks, n - 1)),
        ],
        compiler_params=pltpu.CompilerParams(
            collective_id=0, has_side_effects=True, vmem_limit_bytes=56 * 1024 * 1024
        ),
    )(*operands)
    return pl.pallas_call(
        hand_over,
        out_shape=(
            jax.ShapeDtypeStruct((atoms, ca), BF16),
            jax.ShapeDtypeStruct((tokens, c), BF16),
        ),
    )(final, hidden, atom_token.reshape(1, atoms), bcast_w)


def solution(mesh):
    placed = (
        P(("seed", "tok"), None),
        P("tok", None),
        P("tok"),
        P("tok"),
        P("tok", None, None),
        P(),
        P(),
        P(),
        P(),
        P(),
        P(),
        P(),
    )
    return jax.shard_map(
        local,
        mesh=mesh,
        in_specs=placed,
        out_specs=(P(("seed", "tok"), None), P(("seed", "tok"), None)),
        check_vma=False,
    )
```

```python
import functools

import jax
import jax.numpy as jnp
from jax import lax
from jax.experimental import pallas as pl
from jax.experimental.pallas import tpu as pltpu
from jax.sharding import PartitionSpec as P

H = 16
AH = 4
QW = 32
KW = 128
HALO = 48
SIDE = QW + HALO
EXTRA = 16
F32 = jnp.float32
BF16 = jnp.bfloat16


def layer_norm(values):
    average = jnp.mean(values, axis=-1, keepdims=True)
    centred = values - average
    variance = jnp.mean(centred * centred, axis=-1, keepdims=True)
    return centred * lax.rsqrt(variance + 1e-05)


def dot(a, b):
    return jnp.dot(a, b, preferred_element_type=F32)


def dot_nt(a, b):
    return lax.dot_general(a, b, (((1,), (1,)), ((), ())), preferred_element_type=F32)


def dot_tn(a, b):
    return lax.dot_general(a, b, (((0,), (0,)), ((), ())), preferred_element_type=F32)


def wanted_tokens(tokens, count):
    first = lax.axis_index("tok") * tokens
    row = lax.broadcasted_iota(jnp.int32, (count, 1), 0)
    sides = jnp.where(row == tokens, first - 1, jnp.where(row == tokens + 1, first + tokens, -9))
    return jnp.where(row < tokens, first + row, sides)


def kernel(
    n,
    single_hbm,
    bias_hbm,
    token_hbm,
    pair_hbm,
    qkv_hbm,
    aout_hbm,
    agg_hbm,
    tqkv_hbm,
    tout_hbm,
    pairw_hbm,
    bcast_hbm,
    atom_out,
    token_out,
    xs,
    bs,
    tok_mid,
    tok_low,
    tok_high,
    pair,
    qkv_w,
    aout_w,
    agg_w,
    tqkv_w,
    tout_w,
    pair_w,
    bcast_w,
    proj,
    mixed,
    gathered,
    keyvals,
    pbias,
    local_sem,
    halo_send,
    halo_recv,
    gather_send,
    gather_recv,
    relay_send,
    relay_recv,
):
    atoms, ca = single_hbm.shape
    tokens = pair_hbm.shape[0]
    blocks, c, _ = tout_hbm.shape
    all_tokens = n * tokens
    ext_atoms = atoms + 2 * QW
    ext_tokens = tokens + EXTRA
    used = tokens + 2
    me = lax.axis_index("tok")
    right = lax.rem(me + 1, n)
    left = lax.rem(me + n - 1, n)

    barrier = pltpu.get_barrier_semaphore()
    for k in range(1, n):
        pl.semaphore_signal(
            barrier,
            inc=1,
            device_id={"tok": lax.rem(me + k, n)},
            device_id_type=pl.DeviceIdType.MESH,
        )

    moves = [
        (single_hbm, xs.at[SIDE : SIDE + atoms]),
        (bias_hbm, bs.at[QW : QW + atoms]),
        (token_hbm, tok_mid),
        (qkv_hbm, qkv_w),
        (aout_hbm, aout_w),
        (agg_hbm, agg_w),
        (pairw_hbm, pair_w),
        (pair_hbm, pair.at[0:tokens]),
        (tqkv_hbm.at[0], tqkv_w.at[0]),
        (tout_hbm.at[0], tout_w.at[0]),
        (tqkv_hbm.at[1], tqkv_w.at[1]),
        (tout_hbm.at[1], tout_w.at[1]),
        (bcast_hbm, bcast_w),
    ]
    copies = [
        pltpu.make_async_copy(src, dst, local_sem.at[i]) for i, (src, dst) in enumerate(moves)
    ]
    for copy in copies[:8]:
        copy.start()
    (c_single, c_bias, c_token, c_qkv, c_aout, c_agg, c_pairw, c_pair) = copies[:8]
    c_tqkv = [copies[8], copies[10]]
    c_tout = [copies[9], copies[11]]
    c_bcast = copies[12]

    pl.semaphore_wait(barrier, n - 1)
    halo_moves = [
        (single_hbm.at[atoms - SIDE : atoms], xs.at[0:SIDE], right),
        (single_hbm.at[0:SIDE], xs.at[SIDE + atoms : 2 * SIDE + atoms], left),
        (bias_hbm.at[atoms - QW : atoms], bs.at[0:QW], right),
        (bias_hbm.at[0:QW], bs.at[QW + atoms : 2 * QW + atoms], left),
        (token_hbm, tok_low, right),
        (token_hbm, tok_high, left),
        (pair_hbm.at[tokens - 1], pair.at[tokens], right),
        (pair_hbm.at[0], pair.at[tokens + 1], left),
    ]
    halos = [
        pltpu.make_async_remote_copy(
            src_ref=src,
            dst_ref=dst,
            send_sem=halo_send.at[i],
            recv_sem=halo_recv.at[i],
            device_id={"tok": to},
            device_id_type=pl.DeviceIdType.MESH,
        )
        for i, (src, dst, to) in enumerate(halo_moves)
    ]
    for copy in halos:
        copy.start()
    for copy in copies[8:]:
        copy.start()

    def pair_rows(t):
        rows = dot_nt(pair_w[...], pair[t]).astype(BF16)
        for b in range(blocks):
            pbias[b, t * H : (t + 1) * H, :] = rows[b * H : (b + 1) * H]

    c_single.wait()
    c_bias.wait()
    c_token.wait()
    c_qkv.wait()
    width = ca // AH
    lane = lax.broadcasted_iota(jnp.int32, (QW, ca), 1)
    head_masks = [(lane // width == h).astype(F32) for h in range(AH)]
    head_picks = [m.astype(BF16) for m in head_masks]
    key_lane = lax.broadcasted_iota(jnp.int32, (1, KW), 1)

    def project(rows):
        return dot(layer_norm(rows.astype(F32)).astype(BF16), qkv_w[...]).astype(BF16)

    def window(w):
        q = proj[HALO + QW * w : HALO + QW * (w + 1), :ca]
        keys = proj[QW * w : QW * w + KW, ca : 2 * ca]
        values = proj[QW * w : QW * w + KW, 2 * ca :]
        spread = jnp.concatenate([q * pick for pick in head_picks], axis=0)
        bias = jnp.concatenate(
            [bs[QW * w : QW * (w + 1), h * KW : (h + 1) * KW] for h in range(AH)], axis=0
        )
        scores = dot_nt(spread, keys) * width ** (-0.5) + bias.astype(F32)
        position = me * atoms - SIDE + QW * w + key_lane
        inside = (position >= 0) & (position < n * atoms)
        scores = jnp.where(inside, scores, -1000000000.0)
        powers = jnp.exp(scores - jnp.max(scores, axis=-1, keepdims=True))
        total = jnp.sum(powers, axis=-1, keepdims=True)
        heads = dot(powers.astype(BF16), values) * (1.0 / total)
        out = heads[:QW] * head_masks[0]
        for h in range(1, AH):
            out = out + heads[h * QW : (h + 1) * QW] * head_masks[h]
        mixed[QW * w : QW * (w + 1), :] = out.astype(BF16)

    windows = range(ext_atoms // QW)
    inner = [w for w in windows if QW * w >= SIDE and QW * w + KW <= SIDE + atoms]
    proj[SIDE : SIDE + atoms, :] = project(xs[SIDE : SIDE + atoms])
    for w in inner:
        window(w)
    for copy in halos[:6]:
        copy.wait()
    edges = project(jnp.concatenate([xs[:SIDE], xs[SIDE + atoms :]], axis=0))
    proj[:SIDE, :] = edges[:SIDE]
    proj[SIDE + atoms :, :] = edges[SIDE:]
    for w in windows:
        if w not in inner:
            window(w)
    c_aout.wait()
    c_agg.wait()
    own_rows = xs[HALO : HALO + ext_atoms].astype(F32)
    hidden = (own_rows + dot(mixed[...], aout_w[...])).astype(BF16)
    lifted = jnp.maximum(dot(hidden, agg_w[...]), 0.0)

    wanted = wanted_tokens(tokens, ext_tokens)
    near = jnp.concatenate(
        [tok_low[:, atoms - QW :], tok_mid[...], tok_high[:, :QW]], axis=1
    )
    member = (near == wanted).astype(F32)
    count = jnp.maximum(jnp.sum(member, axis=-1, keepdims=True), 1.0)
    picker = member.astype(BF16)
    upper = lifted.astype(BF16)
    lower = (lifted - upper.astype(F32)).astype(BF16)
    stream = (dot(picker, upper) + dot(picker, lower)) / count

    rows = used * H
    head_size = c // H
    row_token = lax.broadcasted_iota(jnp.int32, (rows, ext_tokens), 0) // H
    spreader = (row_token == lax.broadcasted_iota(jnp.int32, (rows, ext_tokens), 1)).astype(
        F32
    ).astype(BF16)
    col_token = lax.broadcasted_iota(jnp.int32, (ext_tokens, rows), 1) // H
    collector = (col_token == lax.broadcasted_iota(jnp.int32, (ext_tokens, rows), 0)).astype(
        F32
    ).astype(BF16)
    head_row = lax.broadcasted_iota(jnp.int32, (H, c), 0)
    head_lane = lax.broadcasted_iota(jnp.int32, (H, c), 1) // head_size
    tok_mask = (head_row == head_lane).astype(F32).astype(BF16)
    tok_mask = jnp.concatenate([tok_mask] * used, axis=0)
    def flipped(index, bits):
        bit = 1
        while bit <= bits:
            if bits & bit:
                index = index + bit * (1 - 2 * lax.rem(index // bit, 2))
            bit *= 2
        return index

    def shard(index):
        return pl.ds(pl.multiple_of(index * tokens, tokens), tokens)

    def send(b, index, to, send_sem, recv_sem):
        copy = pltpu.make_async_remote_copy(
            src_ref=gathered.at[b, shard(index)],
            dst_ref=gathered.at[b, shard(index)],
            send_sem=send_sem,
            recv_sem=recv_sem,
            device_id={"tok": to},
            device_id_type=pl.DeviceIdType.MESH,
        )
        copy.start()
        return copy

    def project_keyvals(b, indices):
        some = jnp.concatenate([gathered[b, shard(i), :] for i in indices], axis=0)
        result = dot(some, tqkv_w[b, :, c:]).astype(BF16)
        for k, i in enumerate(indices):
            keyvals[shard(i), :] = result[k * tokens : (k + 1) * tokens]

    chips = n // 2
    mate = flipped(me, 1)
    peers = [flipped(me, 2 * j) for j in range(chips)]
    mate_peers = [flipped(mate, 2 * j) for j in range(chips)]
    for b in range(blocks):
        normed = layer_norm(stream).astype(BF16)
        gathered[b, shard(me), :] = normed[:tokens]
        direct = [
            send(b, me, peers[j], gather_send.at[b, j - 1], gather_recv.at[b, j - 1])
            for j in range(1, chips)
        ]
        relays = [send(b, me, mate, relay_send.at[b, 0], relay_recv.at[b, 0])]

        def relay(j):
            direct[j - 1].wait_recv()
            relays.append(send(b, peers[j], mate, relay_send.at[b, j], relay_recv.at[b, j]))

        def queries():
            c_tqkv[b].wait()
            q = dot(normed, tqkv_w[b, :, :c]).astype(BF16)
            return dot(spreader, q).astype(BF16) * tok_mask

        if b == 0:
            c_pairw.wait()
            c_pair.wait()
            for copy in halos[6:]:
                copy.wait()
            for t in range(used // 2):
                pair_rows(t)
            for j in range(1, chips - 1):
                relay(j)
            for t in range(used // 2, used):
                pair_rows(t)
            relay(chips - 1)
            spread = queries()
            relays[0].wait_recv()
            project_keyvals(b, peers[: chips - 1] + mate_peers[:1])
        else:
            spread = queries()
            for j in range(1, chips - 1):
                relay(j)
            relays[0].wait_recv()
            project_keyvals(b, peers[: chips - 1] + mate_peers[:1])
            relay(chips - 1)
        for copy in relays[1:]:
            copy.wait_recv()
        project_keyvals(b, peers[chips - 1 :] + mate_peers[1:])
        for copy in direct + relays:
            copy.wait_send()
        c_tout[b].wait()
        scores = dot_nt(spread, keyvals[:, :c]) * head_size ** (-0.5) + pbias[b].astype(F32)
        powers = jnp.exp(scores - jnp.max(scores, axis=-1, keepdims=True))
        total = jnp.sum(powers, axis=-1, keepdims=True)
        heads = dot(powers.astype(BF16), keyvals[:, c:]) * (1.0 / total)
        update = dot(collector, heads.astype(BF16) * tok_mask).astype(BF16)
        stream = stream + dot(update, tout_w[b])

    final = stream.astype(BF16)
    token_out[...] = final[:tokens]
    c_bcast.wait()
    carry = dot(final, bcast_w[...]).astype(BF16)
    mine = (tok_mid[...] == wanted).astype(F32).astype(BF16)
    atom_out[...] = (hidden[QW : QW + atoms].astype(F32) + dot_tn(mine, carry)).astype(BF16)


def local(
    atom_single,
    atom_bias,
    atom_token,
    atom_counts,
    pair_rep,
    atom_qkv_w,
    atom_out_w,
    agg_w,
    tok_qkv_w,
    tok_out_w,
    pair_w,
    bcast_w,
):
    n = lax.axis_size("tok")
    atoms, ca = atom_single.shape
    tokens, all_tokens, cz = pair_rep.shape
    blocks, c, _ = tok_out_w.shape
    operands = (
        atom_single,
        atom_bias,
        atom_token.reshape(1, atoms),
        pair_rep,
        atom_qkv_w,
        atom_out_w,
        agg_w,
        tok_qkv_w,
        tok_out_w,
        pair_w.T,
        bcast_w,
    )
    dma = pltpu.SemaphoreType.DMA
    return pl.pallas_call(
        functools.partial(kernel, n),
        out_shape=(
            pltpu.VMEM((atoms, ca), BF16),
            pltpu.VMEM((tokens, c), BF16),
        ),
        in_specs=[pl.BlockSpec(memory_space=pltpu.HBM)] * len(operands),
        out_specs=(pl.BlockSpec(memory_space=pltpu.VMEM),) * 2,
        scratch_shapes=[
            pltpu.VMEM((atoms + 2 * SIDE, ca), BF16),
            pltpu.VMEM((atoms + 2 * QW, AH * KW), BF16),
            pltpu.VMEM((1, atoms), jnp.int32),
            pltpu.VMEM((1, atoms), jnp.int32),
            pltpu.VMEM((1, atoms), jnp.int32),
            pltpu.VMEM((tokens + 2, all_tokens, cz), BF16),
            pltpu.VMEM(atom_qkv_w.shape, BF16),
            pltpu.VMEM(atom_out_w.shape, BF16),
            pltpu.VMEM(agg_w.shape, BF16),
            pltpu.VMEM(tok_qkv_w.shape, BF16),
            pltpu.VMEM(tok_out_w.shape, BF16),
            pltpu.VMEM(pair_w.shape[::-1], BF16),
            pltpu.VMEM(bcast_w.shape, BF16),
            pltpu.VMEM((atoms + 2 * SIDE, 3 * ca), BF16),
            pltpu.VMEM((atoms + 2 * QW, ca), BF16),
            pltpu.VMEM((blocks, all_tokens, c), BF16),
            pltpu.VMEM((all_tokens, 2 * c), BF16),
            pltpu.VMEM((blocks, (tokens + 2) * H, all_tokens), BF16),
            dma((13,)),
            dma((8,)),
            dma((8,)),
            dma((blocks, n // 2 - 1)),
            dma((blocks, n // 2 - 1)),
            dma((blocks, n // 2)),
            dma((blocks, n // 2)),
        ],
        compiler_params=pltpu.CompilerParams(
            collective_id=0, has_side_effects=True, vmem_limit_bytes=56 * 1024 * 1024
        ),
    )(*operands)


def solution(mesh):
    placed = (
        P(("seed", "tok"), None),
        P("tok", None),
        P("tok"),
        P("tok"),
        P("tok", None, None),
        P(),
        P(),
        P(),
        P(),
        P(),
        P(),
        P(),
    )
    return jax.shard_map(
        local,
        mesh=mesh,
        in_specs=placed,
        out_specs=(P(("seed", "tok"), None), P(("seed", "tok"), None)),
        check_vma=False,
    )
```

```python
import functools

import jax
import jax.numpy as jnp
from jax import lax
from jax.experimental import pallas as pl
from jax.experimental.pallas import tpu as pltpu
from jax.sharding import PartitionSpec as P

H = 16
AH = 4
QW = 32
KW = 128
HALO = 48
SIDE = QW + HALO
EXTRA = 16
F32 = jnp.float32
BF16 = jnp.bfloat16


def layer_norm(values):
    average = jnp.mean(values, axis=-1, keepdims=True)
    centred = values - average
    variance = jnp.mean(centred * centred, axis=-1, keepdims=True)
    return centred * lax.rsqrt(variance + 1e-05)


def dot(a, b):
    return jnp.dot(a, b, preferred_element_type=F32)


def dot_nt(a, b):
    return lax.dot_general(a, b, (((1,), (1,)), ((), ())), preferred_element_type=F32)


def dot_tn(a, b):
    return lax.dot_general(a, b, (((0,), (0,)), ((), ())), preferred_element_type=F32)


def wanted_tokens(tokens, count):
    first = lax.axis_index("tok") * tokens
    row = lax.broadcasted_iota(jnp.int32, (count, 1), 0)
    sides = jnp.where(row == tokens, first - 1, jnp.where(row == tokens + 1, first + tokens, -9))
    return jnp.where(row < tokens, first + row, sides)


def kernel(
    n,
    single_hbm,
    bias_hbm,
    token_hbm,
    pair_hbm,
    qkv_hbm,
    aout_hbm,
    agg_hbm,
    tqkv_hbm,
    tout_hbm,
    pairw_hbm,
    bcast_hbm,
    atom_out,
    token_out,
    xs,
    bs,
    tok_mid,
    tok_low,
    tok_high,
    pair,
    qkv_w,
    aout_w,
    agg_w,
    tqkv_w,
    tout_w,
    pair_w,
    bcast_w,
    proj,
    mixed,
    gathered,
    keyvals,
    pbias,
    local_sem,
    halo_send,
    halo_recv,
    gather_send,
    gather_recv,
    relay_send,
    relay_recv,
):
    atoms, ca = single_hbm.shape
    tokens = pair_hbm.shape[0]
    blocks, c, _ = tout_hbm.shape
    all_tokens = n * tokens
    ext_atoms = atoms + 2 * QW
    ext_tokens = tokens + EXTRA
    used = tokens + 2
    me = lax.axis_index("tok")
    right = lax.rem(me + 1, n)
    left = lax.rem(me + n - 1, n)

    barrier = pltpu.get_barrier_semaphore()
    for k in range(1, n):
        pl.semaphore_signal(
            barrier,
            inc=1,
            device_id={"tok": lax.rem(me + k, n)},
            device_id_type=pl.DeviceIdType.MESH,
        )

    moves = [
        (single_hbm, xs.at[SIDE : SIDE + atoms]),
        (bias_hbm, bs.at[QW : QW + atoms]),
        (token_hbm, tok_mid),
        (qkv_hbm, qkv_w),
        (aout_hbm, aout_w),
        (agg_hbm, agg_w),
        (pairw_hbm, pair_w),
        (pair_hbm, pair.at[0:tokens]),
        (tqkv_hbm.at[0], tqkv_w.at[0]),
        (tout_hbm.at[0], tout_w.at[0]),
        (tqkv_hbm.at[1], tqkv_w.at[1]),
        (tout_hbm.at[1], tout_w.at[1]),
        (bcast_hbm, bcast_w),
    ]
    copies = [
        pltpu.make_async_copy(src, dst, local_sem.at[i]) for i, (src, dst) in enumerate(moves)
    ]
    for copy in copies[:8]:
        copy.start()
    (c_single, c_bias, c_token, c_qkv, c_aout, c_agg, c_pairw, c_pair) = copies[:8]
    c_tqkv = [copies[8], copies[10]]
    c_tout = [copies[9], copies[11]]
    c_bcast = copies[12]

    def flipped(index, bits):
        bit = 1
        while bit <= bits:
            if bits & bit:
                index = index + bit * (1 - 2 * lax.rem(lax.div(index, bit), 2))
            bit *= 2
        return index

    chips = n // 2
    mate = flipped(me, 1)
    peers = [flipped(me, 2 * j) for j in range(chips)]
    mate_peers = [flipped(mate, 2 * j) for j in range(chips)]

    def between(shape, dim, size):
        offset = lax.broadcasted_iota(jnp.int32, shape, 1 - dim) - size * lax.broadcasted_iota(
            jnp.int32, shape, dim
        )
        return ((offset >= 0) & (offset < size)).astype(F32)

    width = ca // AH
    rows = used * H
    head_size = c // H
    lane = lax.broadcasted_iota(jnp.int32, (QW, ca), 1)
    head_masks = [
        ((lane >= width * h) & (lane < width * (h + 1))).astype(F32) for h in range(AH)
    ]
    head_picks = [m.astype(BF16) for m in head_masks]
    key_lane = lax.broadcasted_iota(jnp.int32, (1, KW), 1)
    spreader = between((rows, ext_tokens), 1, H).astype(BF16)
    collector = between((ext_tokens, rows), 0, H).astype(BF16)
    tok_mask = between((H, c), 0, head_size).astype(BF16)
    tok_mask = jnp.concatenate([tok_mask] * used, axis=0)

    pl.semaphore_wait(barrier, n - 1)
    halo_moves = [
        (single_hbm.at[atoms - SIDE : atoms], xs.at[0:SIDE], right),
        (single_hbm.at[0:SIDE], xs.at[SIDE + atoms : 2 * SIDE + atoms], left),
        (bias_hbm.at[atoms - QW : atoms], bs.at[0:QW], right),
        (bias_hbm.at[0:QW], bs.at[QW + atoms : 2 * QW + atoms], left),
        (token_hbm, tok_low, right),
        (token_hbm, tok_high, left),
        (pair_hbm.at[tokens - 1], pair.at[tokens], right),
        (pair_hbm.at[0], pair.at[tokens + 1], left),
    ]
    halos = [
        pltpu.make_async_remote_copy(
            src_ref=src,
            dst_ref=dst,
            send_sem=halo_send.at[i],
            recv_sem=halo_recv.at[i],
            device_id={"tok": to},
            device_id_type=pl.DeviceIdType.MESH,
        )
        for i, (src, dst, to) in enumerate(halo_moves)
    ]
    for copy in halos:
        copy.start()
    for copy in copies[8:]:
        copy.start()

    def pair_rows(t):
        weight = pair_w[...]
        blank = jnp.zeros_like(weight)
        both = jnp.concatenate(
            [
                jnp.concatenate([weight, blank], axis=1),
                jnp.concatenate([blank, weight], axis=1),
            ],
            axis=0,
        )
        duo = jnp.concatenate([pair[t], pair[t + 1]], axis=1)
        rows = dot_nt(both, duo).astype(BF16)
        for k in range(2):
            for b in range(blocks):
                at = (k * blocks + b) * H
                pbias[b, (t + k) * H : (t + k + 1) * H, :] = rows[at : at + H]

    c_single.wait()
    c_bias.wait()
    c_token.wait()
    c_qkv.wait()

    def project(rows):
        return dot(layer_norm(rows.astype(F32)).astype(BF16), qkv_w[...]).astype(BF16)

    def attend(some, masked):
        scores = []
        for w in some:
            q = proj[HALO + QW * w : HALO + QW * (w + 1), :ca]
            keys = proj[QW * w : QW * w + KW, ca : 2 * ca]
            spread = jnp.concatenate([q * pick for pick in head_picks], axis=0)
            scores.append(dot_nt(spread, keys))
        for i, w in enumerate(some):
            bias = jnp.concatenate(
                [bs[QW * w : QW * (w + 1), h * KW : (h + 1) * KW] for h in range(AH)], axis=0
            )
            scores[i] = scores[i] * width ** (-0.5) + bias.astype(F32)
            if masked:
                position = me * atoms - SIDE + QW * w + key_lane
                inside = (position >= 0) & (position < n * atoms)
                scores[i] = jnp.where(inside, scores[i], -1000000000.0)
        maxima = [jnp.max(x, axis=-1, keepdims=True) for x in scores]
        powers = [jnp.exp(x - m) for x, m in zip(scores, maxima)]
        totals = [jnp.sum(x, axis=-1, keepdims=True) for x in powers]
        heads = [
            dot(x.astype(BF16), proj[QW * w : QW * w + KW, 2 * ca :])
            for w, x in zip(some, powers)
        ]
        for w, x, total in zip(some, heads, totals):
            x = x * (1.0 / total)
            out = x[:QW] * head_masks[0]
            for h in range(1, AH):
                out = out + x[h * QW : (h + 1) * QW] * head_masks[h]
            mixed[QW * w : QW * (w + 1), :] = out.astype(BF16)

    windows = range(ext_atoms // QW)
    inner = [w for w in windows if QW * w >= SIDE and QW * w + KW <= SIDE + atoms]
    proj[SIDE : SIDE + atoms, :] = project(xs[SIDE : SIDE + atoms])
    attend(inner, False)
    for copy in halos[:6]:
        copy.wait()
    edges = project(jnp.concatenate([xs[:SIDE], xs[SIDE + atoms :]], axis=0))
    proj[:SIDE, :] = edges[:SIDE]
    proj[SIDE + atoms :, :] = edges[SIDE:]
    attend([w for w in windows if w not in inner], True)
    c_aout.wait()
    c_agg.wait()
    own_rows = xs[HALO : HALO + ext_atoms].astype(F32)
    hidden = (own_rows + dot(mixed[...], aout_w[...])).astype(BF16)
    lifted = jnp.maximum(dot(hidden, agg_w[...]), 0.0)

    wanted = wanted_tokens(tokens, ext_tokens)
    near = jnp.concatenate(
        [tok_low[:, atoms - QW :], tok_mid[...], tok_high[:, :QW]], axis=1
    )
    member = (near == wanted).astype(F32)
    count = jnp.maximum(jnp.sum(member, axis=-1, keepdims=True), 1.0)
    picker = member.astype(BF16)
    upper = lifted.astype(BF16)
    lower = (lifted - upper.astype(F32)).astype(BF16)
    stream = (dot(picker, upper) + dot(picker, lower)) / count

    def shard(index):
        return pl.ds(pl.multiple_of(index * tokens, tokens), tokens)

    def send(b, index, to, send_sem, recv_sem):
        copy = pltpu.make_async_remote_copy(
            src_ref=gathered.at[b, shard(index)],
            dst_ref=gathered.at[b, shard(index)],
            send_sem=send_sem,
            recv_sem=recv_sem,
            device_id={"tok": to},
            device_id_type=pl.DeviceIdType.MESH,
        )
        copy.start()
        return copy

    def project_keyvals(b, indices):
        some = jnp.concatenate([gathered[b, shard(i), :] for i in indices], axis=0)
        result = dot(some, tqkv_w[b, :, c:]).astype(BF16)
        for k, i in enumerate(indices):
            keyvals[shard(i), :] = result[k * tokens : (k + 1) * tokens]

    for b in range(blocks):
        normed = layer_norm(stream).astype(BF16)
        gathered[b, shard(me), :] = normed[:tokens]
        direct = [
            send(b, me, peers[j], gather_send.at[b, j - 1], gather_recv.at[b, j - 1])
            for j in range(1, chips)
        ]
        relays = [send(b, me, mate, relay_send.at[b, 0], relay_recv.at[b, 0])]

        def relay(j):
            direct[j - 1].wait_recv()
            relays.append(send(b, peers[j], mate, relay_send.at[b, j], relay_recv.at[b, j]))

        def queries():
            c_tqkv[b].wait()
            q = dot(normed, tqkv_w[b, :, :c]).astype(BF16)
            return dot(spreader, q).astype(BF16) * tok_mask

        if b == 0:
            c_pairw.wait()
            c_pair.wait()
            for copy in halos[6:]:
                copy.wait()
            half = used // 4 * 2
            for t in range(0, half, 2):
                pair_rows(t)
            for j in range(1, chips - 1):
                relay(j)
            for t in range(half, used, 2):
                pair_rows(t)
            relay(chips - 1)
            spread = queries()
            relays[0].wait_recv()
            project_keyvals(b, peers[: chips - 1] + mate_peers[:1])
        else:
            spread = queries()
            for j in range(1, chips - 1):
                relay(j)
            relays[0].wait_recv()
            project_keyvals(b, peers[: chips - 1] + mate_peers[:1])
            relay(chips - 1)
        for copy in relays[1:]:
            copy.wait_recv()
        project_keyvals(b, peers[chips - 1 :] + mate_peers[1:])
        for copy in direct + relays:
            copy.wait_send()
        c_tout[b].wait()
        scores = dot_nt(spread, keyvals[:, :c]) * head_size ** (-0.5) + pbias[b].astype(F32)
        powers = jnp.exp(scores - jnp.max(scores, axis=-1, keepdims=True))
        total = jnp.sum(powers, axis=-1, keepdims=True)
        heads = dot(powers.astype(BF16), keyvals[:, c:]) * (1.0 / total)
        update = dot(collector, heads.astype(BF16) * tok_mask).astype(BF16)
        stream = stream + dot(update, tout_w[b])

    final = stream.astype(BF16)
    token_out[...] = final[:tokens]
    c_bcast.wait()
    carry = dot(final, bcast_w[...]).astype(BF16)
    mine = (tok_mid[...] == wanted).astype(F32).astype(BF16)
    atom_out[...] = (hidden[QW : QW + atoms].astype(F32) + dot_tn(mine, carry)).astype(BF16)


def local(
    atom_single,
    atom_bias,
    atom_token,
    atom_counts,
    pair_rep,
    atom_qkv_w,
    atom_out_w,
    agg_w,
    tok_qkv_w,
    tok_out_w,
    pair_w,
    bcast_w,
):
    n = lax.axis_size("tok")
    atoms, ca = atom_single.shape
    tokens, all_tokens, cz = pair_rep.shape
    blocks, c, _ = tok_out_w.shape
    operands = (
        atom_single,
        atom_bias,
        atom_token.reshape(1, atoms),
        pair_rep,
        atom_qkv_w,
        atom_out_w,
        agg_w,
        tok_qkv_w,
        tok_out_w,
        pair_w.T,
        bcast_w,
    )
    dma = pltpu.SemaphoreType.DMA
    return pl.pallas_call(
        functools.partial(kernel, n),
        out_shape=(
            pltpu.VMEM((atoms, ca), BF16),
            pltpu.VMEM((tokens, c), BF16),
        ),
        in_specs=[pl.BlockSpec(memory_space=pltpu.HBM)] * len(operands),
        out_specs=(pl.BlockSpec(memory_space=pltpu.VMEM),) * 2,
        scratch_shapes=[
            pltpu.VMEM((atoms + 2 * SIDE, ca), BF16),
            pltpu.VMEM((atoms + 2 * QW, AH * KW), BF16),
            pltpu.VMEM((1, atoms), jnp.int32),
            pltpu.VMEM((1, atoms), jnp.int32),
            pltpu.VMEM((1, atoms), jnp.int32),
            pltpu.VMEM((tokens + 2, all_tokens, cz), BF16),
            pltpu.VMEM(atom_qkv_w.shape, BF16),
            pltpu.VMEM(atom_out_w.shape, BF16),
            pltpu.VMEM(agg_w.shape, BF16),
            pltpu.VMEM(tok_qkv_w.shape, BF16),
            pltpu.VMEM(tok_out_w.shape, BF16),
            pltpu.VMEM(pair_w.shape[::-1], BF16),
            pltpu.VMEM(bcast_w.shape, BF16),
            pltpu.VMEM((atoms + 2 * SIDE, 3 * ca), BF16),
            pltpu.VMEM((atoms + 2 * QW, ca), BF16),
            pltpu.VMEM((blocks, all_tokens, c), BF16),
            pltpu.VMEM((all_tokens, 2 * c), BF16),
            pltpu.VMEM((blocks, (tokens + 2) * H, all_tokens), BF16),
            dma((13,)),
            dma((8,)),
            dma((8,)),
            dma((blocks, n // 2 - 1)),
            dma((blocks, n // 2 - 1)),
            dma((blocks, n // 2)),
            dma((blocks, n // 2)),
        ],
        compiler_params=pltpu.CompilerParams(
            collective_id=0, has_side_effects=True, vmem_limit_bytes=56 * 1024 * 1024
        ),
    )(*operands)


def solution(mesh):
    placed = (
        P(("seed", "tok"), None),
        P("tok", None),
        P("tok"),
        P("tok"),
        P("tok", None, None),
        P(),
        P(),
        P(),
        P(),
        P(),
        P(),
        P(),
    )
    return jax.shard_map(
        local,
        mesh=mesh,
        in_specs=placed,
        out_specs=(P(("seed", "tok"), None), P(("seed", "tok"), None)),
        check_vma=False,
    )
```

```python
import functools

import jax
import jax.numpy as jnp
from jax import lax
from jax.experimental import pallas as pl
from jax.experimental.pallas import tpu as pltpu
from jax.sharding import PartitionSpec as P

H = 16
AH = 4
QW = 32
KW = 128
HALO = 48
SIDE = QW + HALO
EXTRA = 16
F32 = jnp.float32
BF16 = jnp.bfloat16


def layer_norm(values):
    average = jnp.mean(values, axis=-1, keepdims=True)
    centred = values - average
    variance = jnp.mean(centred * centred, axis=-1, keepdims=True)
    return centred * lax.rsqrt(variance + 1e-05)


def dot(a, b):
    return jnp.dot(a, b, preferred_element_type=F32)


def dot_nt(a, b):
    return lax.dot_general(a, b, (((1,), (1,)), ((), ())), preferred_element_type=F32)


def dot_tn(a, b):
    return lax.dot_general(a, b, (((0,), (0,)), ((), ())), preferred_element_type=F32)


def wanted_tokens(tokens, count):
    first = lax.axis_index("tok") * tokens
    row = lax.broadcasted_iota(jnp.int32, (count, 1), 0)
    sides = jnp.where(row == tokens, first - 1, jnp.where(row == tokens + 1, first + tokens, -9))
    return jnp.where(row < tokens, first + row, sides)


def kernel(
    n,
    single_hbm,
    bias_hbm,
    token_hbm,
    pair_hbm,
    qkv_hbm,
    aout_hbm,
    agg_hbm,
    tqkv_hbm,
    tout_hbm,
    pairw_hbm,
    bcast_hbm,
    atom_out,
    token_out,
    xs,
    bs,
    tok_mid,
    tok_low,
    tok_high,
    pair,
    qkv_w,
    aout_w,
    agg_w,
    tqkv_w,
    tout_w,
    pair_w,
    bcast_w,
    proj,
    mixed,
    gathered,
    pbias,
    local_sem,
    halo_send,
    halo_recv,
    gather_send,
    gather_recv,
    relay_send,
    relay_recv,
):
    atoms, ca = single_hbm.shape
    tokens = pair_hbm.shape[0]
    blocks, c, _ = tout_hbm.shape
    all_tokens = n * tokens
    ext_atoms = atoms + 2 * QW
    ext_tokens = tokens + EXTRA
    used = tokens + 2
    me = lax.axis_index("tok")
    right = lax.rem(me + 1, n)
    left = lax.rem(me + n - 1, n)

    barrier = pltpu.get_barrier_semaphore()
    for k in range(1, n):
        pl.semaphore_signal(
            barrier,
            inc=1,
            device_id={"tok": lax.rem(me + k, n)},
            device_id_type=pl.DeviceIdType.MESH,
        )

    moves = [
        (single_hbm, xs.at[SIDE : SIDE + atoms]),
        (bias_hbm, bs.at[QW : QW + atoms]),
        (token_hbm, tok_mid),
        (qkv_hbm, qkv_w),
        (aout_hbm, aout_w),
        (agg_hbm, agg_w),
        (pairw_hbm, pair_w),
        (pair_hbm, pair.at[0:tokens]),
        (tqkv_hbm.at[0], tqkv_w.at[0]),
        (tout_hbm.at[0], tout_w.at[0]),
        (tqkv_hbm.at[1], tqkv_w.at[1]),
        (tout_hbm.at[1], tout_w.at[1]),
        (bcast_hbm, bcast_w),
    ]
    copies = [
        pltpu.make_async_copy(src, dst, local_sem.at[i]) for i, (src, dst) in enumerate(moves)
    ]
    for copy in copies[:8]:
        copy.start()
    (c_single, c_bias, c_token, c_qkv, c_aout, c_agg, c_pairw, c_pair) = copies[:8]
    c_tqkv = [copies[8], copies[10]]
    c_tout = [copies[9], copies[11]]
    c_bcast = copies[12]

    def flipped(index, bits):
        bit = 1
        while bit <= bits:
            if bits & bit:
                index = index + bit * (1 - 2 * lax.rem(lax.div(index, bit), 2))
            bit *= 2
        return index

    chips = n // 2
    mate = flipped(me, 1)
    peers = [flipped(me, 2 * j) for j in range(chips)]

    def between(shape, dim, size):
        offset = lax.broadcasted_iota(jnp.int32, shape, 1 - dim) - size * lax.broadcasted_iota(
            jnp.int32, shape, dim
        )
        return ((offset >= 0) & (offset < size)).astype(F32)

    width = ca // AH
    rows = used * H
    head_size = c // H
    lane = lax.broadcasted_iota(jnp.int32, (QW, ca), 1)
    head_masks = [
        ((lane >= width * h) & (lane < width * (h + 1))).astype(F32) for h in range(AH)
    ]
    head_picks = [m.astype(BF16) for m in head_masks]
    key_lane = lax.broadcasted_iota(jnp.int32, (1, KW), 1)
    spreader = between((rows, ext_tokens), 1, H).astype(BF16)
    collector = between((ext_tokens, rows), 0, H).astype(BF16)
    tok_mask = between((H, c), 0, head_size).astype(BF16)
    tok_mask = jnp.concatenate([tok_mask] * used, axis=0)

    pl.semaphore_wait(barrier, n - 1)
    halo_moves = [
        (single_hbm.at[atoms - SIDE : atoms], xs.at[0:SIDE], right),
        (single_hbm.at[0:SIDE], xs.at[SIDE + atoms : 2 * SIDE + atoms], left),
        (bias_hbm.at[atoms - QW : atoms], bs.at[0:QW], right),
        (bias_hbm.at[0:QW], bs.at[QW + atoms : 2 * QW + atoms], left),
        (token_hbm, tok_low, right),
        (token_hbm, tok_high, left),
        (pair_hbm.at[tokens - 1], pair.at[tokens], right),
        (pair_hbm.at[0], pair.at[tokens + 1], left),
    ]
    halos = [
        pltpu.make_async_remote_copy(
            src_ref=src,
            dst_ref=dst,
            send_sem=halo_send.at[i],
            recv_sem=halo_recv.at[i],
            device_id={"tok": to},
            device_id_type=pl.DeviceIdType.MESH,
        )
        for i, (src, dst, to) in enumerate(halo_moves)
    ]
    for copy in halos:
        copy.start()
    for copy in copies[8:]:
        copy.start()

    def pair_rows(t):
        weight = pair_w[...]
        blank = jnp.zeros_like(weight)
        both = jnp.concatenate(
            [
                jnp.concatenate([weight, blank], axis=1),
                jnp.concatenate([blank, weight], axis=1),
            ],
            axis=0,
        )
        duo = jnp.concatenate([pair[t], pair[t + 1]], axis=1)
        rows = dot_nt(both, duo).astype(BF16)
        for k in range(2):
            for b in range(blocks):
                at = (k * blocks + b) * H
                pbias[b, (t + k) * H : (t + k + 1) * H, :] = rows[at : at + H]

    c_single.wait()
    c_bias.wait()
    c_token.wait()
    c_qkv.wait()

    def project(rows):
        return dot(layer_norm(rows.astype(F32)).astype(BF16), qkv_w[...]).astype(BF16)

    def attend(some, masked):
        scores = []
        for w in some:
            q = proj[HALO + QW * w : HALO + QW * (w + 1), :ca]
            keys = proj[QW * w : QW * w + KW, ca : 2 * ca]
            spread = jnp.concatenate([q * pick for pick in head_picks], axis=0)
            scores.append(dot_nt(spread, keys))
        for i, w in enumerate(some):
            bias = jnp.concatenate(
                [bs[QW * w : QW * (w + 1), h * KW : (h + 1) * KW] for h in range(AH)], axis=0
            )
            scores[i] = scores[i] * width ** (-0.5) + bias.astype(F32)
            if masked:
                position = me * atoms - SIDE + QW * w + key_lane
                inside = (position >= 0) & (position < n * atoms)
                scores[i] = jnp.where(inside, scores[i], -1000000000.0)
        maxima = [jnp.max(x, axis=-1, keepdims=True) for x in scores]
        powers = [jnp.exp(x - m) for x, m in zip(scores, maxima)]
        totals = [jnp.sum(x, axis=-1, keepdims=True) for x in powers]
        heads = [
            dot(x.astype(BF16), proj[QW * w : QW * w + KW, 2 * ca :])
            for w, x in zip(some, powers)
        ]
        for w, x, total in zip(some, heads, totals):
            x = x * (1.0 / total)
            out = x[:QW] * head_masks[0]
            for h in range(1, AH):
                out = out + x[h * QW : (h + 1) * QW] * head_masks[h]
            mixed[QW * w : QW * (w + 1), :] = out.astype(BF16)

    windows = range(ext_atoms // QW)
    inner = [w for w in windows if QW * w >= SIDE and QW * w + KW <= SIDE + atoms]
    proj[SIDE : SIDE + atoms, :] = project(xs[SIDE : SIDE + atoms])
    attend(inner, False)
    for copy in halos[:6]:
        copy.wait()
    edges = project(jnp.concatenate([xs[:SIDE], xs[SIDE + atoms :]], axis=0))
    proj[:SIDE, :] = edges[:SIDE]
    proj[SIDE + atoms :, :] = edges[SIDE:]
    attend([w for w in windows if w not in inner], True)
    c_aout.wait()
    c_agg.wait()
    own_rows = xs[HALO : HALO + ext_atoms].astype(F32)
    hidden = (own_rows + dot(mixed[...], aout_w[...])).astype(BF16)
    lifted = jnp.maximum(dot(hidden, agg_w[...]), 0.0)

    wanted = wanted_tokens(tokens, ext_tokens)
    near = jnp.concatenate(
        [tok_low[:, atoms - QW :], tok_mid[...], tok_high[:, :QW]], axis=1
    )
    member = (near == wanted).astype(F32)
    count = jnp.maximum(jnp.sum(member, axis=-1, keepdims=True), 1.0)
    picker = member.astype(BF16)
    upper = lifted.astype(BF16)
    lower = (lifted - upper.astype(F32)).astype(BF16)
    stream = (dot(picker, upper) + dot(picker, lower)) / count

    def shard(index):
        return pl.ds(pl.multiple_of(index * tokens, tokens), tokens)

    def send(b, index, to, send_sem, recv_sem):
        copy = pltpu.make_async_remote_copy(
            src_ref=gathered.at[b, shard(index)],
            dst_ref=gathered.at[b, shard(index)],
            send_sem=send_sem,
            recv_sem=recv_sem,
            device_id={"tok": to},
            device_id_type=pl.DeviceIdType.MESH,
        )
        copy.start()
        return copy

    for b in range(blocks):
        normed = layer_norm(stream).astype(BF16)
        gathered[b, shard(me), :] = normed[:tokens]
        direct = [
            send(b, me, peers[j], gather_send.at[b, j - 1], gather_recv.at[b, j - 1])
            for j in range(1, chips)
        ]
        relays = [send(b, me, mate, relay_send.at[b, 0], relay_recv.at[b, 0])]

        def relay(j):
            direct[j - 1].wait_recv()
            relays.append(send(b, peers[j], mate, relay_send.at[b, j], relay_recv.at[b, j]))

        def queries():
            c_tqkv[b].wait()
            q = dot(normed, tqkv_w[b, :, :c]).astype(BF16)
            return dot(spreader, q).astype(BF16) * tok_mask

        if b == 0:
            c_pairw.wait()
            c_pair.wait()
            for copy in halos[6:]:
                copy.wait()
            half = used // 4 * 2
            for t in range(0, half, 2):
                pair_rows(t)
            for j in range(1, chips - 1):
                relay(j)
            for t in range(half, used, 2):
                pair_rows(t)
            relay(chips - 1)
            spread = queries()
        else:
            spread = queries()
            for j in range(1, chips):
                relay(j)
        for copy in relays:
            copy.wait_recv()
        c_tout[b].wait()
        everyone = gathered[b]
        keys = dot(everyone, tqkv_w[b, :, c : 2 * c]).astype(BF16)
        scores = dot_nt(spread, keys) * head_size ** (-0.5) + pbias[b].astype(F32)
        powers = jnp.exp(scores - jnp.max(scores, axis=-1, keepdims=True))
        total = jnp.sum(powers, axis=-1, keepdims=True)
        values = dot(everyone, tqkv_w[b, :, 2 * c :]).astype(BF16)
        heads = dot(powers.astype(BF16), values) * (1.0 / total)
        update = dot(collector, heads.astype(BF16) * tok_mask).astype(BF16)
        stream = stream + dot(update, tout_w[b])
        for copy in direct + relays:
            copy.wait_send()

    final = stream.astype(BF16)
    token_out[...] = final[:tokens]
    c_bcast.wait()
    carry = dot(final, bcast_w[...]).astype(BF16)
    mine = (tok_mid[...] == wanted).astype(F32).astype(BF16)
    atom_out[...] = (hidden[QW : QW + atoms].astype(F32) + dot_tn(mine, carry)).astype(BF16)


def local(
    atom_single,
    atom_bias,
    atom_token,
    atom_counts,
    pair_rep,
    atom_qkv_w,
    atom_out_w,
    agg_w,
    tok_qkv_w,
    tok_out_w,
    pair_w,
    bcast_w,
):
    n = lax.axis_size("tok")
    atoms, ca = atom_single.shape
    tokens, all_tokens, cz = pair_rep.shape
    blocks, c, _ = tok_out_w.shape
    operands = (
        atom_single,
        atom_bias,
        atom_token.reshape(1, atoms),
        pair_rep,
        atom_qkv_w,
        atom_out_w,
        agg_w,
        tok_qkv_w,
        tok_out_w,
        pair_w.T,
        bcast_w,
    )
    dma = pltpu.SemaphoreType.DMA
    return pl.pallas_call(
        functools.partial(kernel, n),
        out_shape=(
            pltpu.VMEM((atoms, ca), BF16),
            pltpu.VMEM((tokens, c), BF16),
        ),
        in_specs=[pl.BlockSpec(memory_space=pltpu.HBM)] * len(operands),
        out_specs=(pl.BlockSpec(memory_space=pltpu.VMEM),) * 2,
        scratch_shapes=[
            pltpu.VMEM((atoms + 2 * SIDE, ca), BF16),
            pltpu.VMEM((atoms + 2 * QW, AH * KW), BF16),
            pltpu.VMEM((1, atoms), jnp.int32),
            pltpu.VMEM((1, atoms), jnp.int32),
            pltpu.VMEM((1, atoms), jnp.int32),
            pltpu.VMEM((tokens + 2, all_tokens, cz), BF16),
            pltpu.VMEM(atom_qkv_w.shape, BF16),
            pltpu.VMEM(atom_out_w.shape, BF16),
            pltpu.VMEM(agg_w.shape, BF16),
            pltpu.VMEM(tok_qkv_w.shape, BF16),
            pltpu.VMEM(tok_out_w.shape, BF16),
            pltpu.VMEM(pair_w.shape[::-1], BF16),
            pltpu.VMEM(bcast_w.shape, BF16),
            pltpu.VMEM((atoms + 2 * SIDE, 3 * ca), BF16),
            pltpu.VMEM((atoms + 2 * QW, ca), BF16),
            pltpu.VMEM((blocks, all_tokens, c), BF16),
            pltpu.VMEM((blocks, (tokens + 2) * H, all_tokens), BF16),
            dma((13,)),
            dma((8,)),
            dma((8,)),
            dma((blocks, n // 2 - 1)),
            dma((blocks, n // 2 - 1)),
            dma((blocks, n // 2)),
            dma((blocks, n // 2)),
        ],
        compiler_params=pltpu.CompilerParams(
            collective_id=0, has_side_effects=True, vmem_limit_bytes=56 * 1024 * 1024
        ),
    )(*operands)


def solution(mesh):
    placed = (
        P(("seed", "tok"), None),
        P("tok", None),
        P("tok"),
        P("tok"),
        P("tok", None, None),
        P(),
        P(),
        P(),
        P(),
        P(),
        P(),
        P(),
    )
    return jax.shard_map(
        local,
        mesh=mesh,
        in_specs=placed,
        out_specs=(P(("seed", "tok"), None), P(("seed", "tok"), None)),
        check_vma=False,
    )
```
